32 devices in a mesh: section: 2 (over x), ctx: 4 (over z), mp: 4 (over y, core).
Axes of the slice: x: 2, y: 2, z: 4, core: 2. Of those that a mesh axis runs over, the one named last changes fastest.
Arguments:
- queries: bfloat16 [2, 1024, 4096], P('section', 'ctx', 'mp'), may hold values from -130 to 130
- keys: bfloat16 [2, 1024, 512], P('section', 'ctx', 'mp'), may hold values from -4.5 to 4.5
- values: bfloat16 [2, 1024, 512], P('section', 'ctx', 'mp'), may hold values from -6 to 6
- doc_lengths: int32 [2, 16], P('section'), may hold values from 1 to 512, 1024 in all within a row
Outputs:
- attended: bfloat16 [2, 1024, 4096], P('section', ('ctx', 'mp'))
- passed: bfloat16 [2, 1024, 4096], P('section', ('ctx', 'mp'))
The draws below stay inside these ranges and needn't reach their ends.
All inputs are finite; a program needn't handle non-finite values.
Results may differ from the reference program's by a relative error of at most 0.004.
Values may be sent and summed in bfloat16 or wider, within the bound.
A program may use at most 192 MiB of HBM per device.

```python
import math
import jax
import jax.numpy as jnp
import numpy as np
from jax import lax

DH = 128
QH = 32
KVH = 4
DOCS = 16
SECTIONS = 2
TOKENS = 1024
MOST = 512
LOGN_BASE = 64


def shared_rows(key):
    base = jax.random.fold_in(key, 11)
    first = jax.random.fold_in(base, 0)
    key_base = jnp.clip(jax.random.normal(first, (SECTIONS, TOKENS, KVH, DH), jnp.float32), -4.0, 4.0)
    final_keys = key_base
    return final_keys


def draw_keys(key, part):
    final_keys = shared_rows(key)
    return final_keys.reshape(SECTIONS, TOKENS, KVH * DH).astype(jnp.bfloat16)


def draw_queries(key, part):
    query_key = jax.random.fold_in(key, 23)
    query_base = jnp.clip(jax.random.normal(query_key, (SECTIONS, TOKENS, QH, DH), jnp.float32), -6.0, 6.0)
    result = query_base
    return result.reshape(SECTIONS, TOKENS, QH * DH).astype(jnp.bfloat16)


def block_levels(own_key, dims, cuts, least, largest):
    loudness, own = 1.0, jax.random.fold_in(own_key, 6)
    for position, shards_of in cuts:
        heights = jnp.exp(jax.random.uniform(jax.random.fold_in(own, position), (shards_of,), jnp.float32, least / len(cuts), largest / len(cuts)))
        loudness = loudness * jnp.repeat(heights, dims[position] // shards_of).reshape([-1 if axis == position else 1 for axis in range(len(dims))])
    return loudness


def length_profile(count, total, bound, skew):
    loads = [(1 << 20) // math.isqrt(standing ** skew) + 1 for standing in range(2, count + 1)]
    surplus, counts = total - bound - (count - 1), [1] * (count - 1)
    while surplus > 0:
        free = [i for i in range(count - 1) if counts[i] < bound]
        mass, budget = sum([loads[i] for i in free]), surplus
        for i in free:
            extra = min(bound - counts[i], max(1, budget * loads[i] // mass), surplus)
            counts[i] = counts[i] + extra
            surplus = surplus - extra
    return np.array([bound] + counts)


def uneven(own_key, number_of, total, limit, slope):
    if number_of == 2:
        one = jax.random.randint(own_key, (), max(1, total - limit), min(limit, total - 1) + 1)
        return jnp.stack([one, total - one])
    sizes = jnp.asarray(length_profile(number_of, total, limit, slope), jnp.int32)
    pairs = (number_of - 1) // 2
    giver, sink = sizes[1:1 + 2 * pairs:2], sizes[2:2 + 2 * pairs:2]
    margin = jnp.minimum(giver - 1, limit - sink)
    moved = jax.random.randint(jax.random.fold_in(own_key, 1), (pairs,), 0, 1 << 20) % (margin + 1)
    sizes = sizes.at[1:1 + 2 * pairs:2].set(giver - moved).at[2:2 + 2 * pairs:2].set(sink + moved)
    return sizes[jax.random.permutation(jax.random.fold_in(own_key, 2), number_of)]


def normal_values(own_key, dims, spread, reach, cuts=(), held_as=jnp.bfloat16):
    level = block_levels(own_key, dims, cuts, -0.22, 0.18) if cuts else 1.0
    drawn = jax.random.normal(own_key, dims, jnp.float32) * spread * level
    return jnp.minimum(jnp.maximum(drawn, -reach), reach).astype(held_as)


def setup_inputs(seed: int = 0) -> dict:
    streams_of = jax.random.split(jax.random.key(seed), 5)
    queries = draw_queries(jax.random.fold_in(streams_of[4], 71), 0)
    keys = draw_keys(jax.random.fold_in(streams_of[4], 71), 0)
    values = normal_values(streams_of[2], (SECTIONS, TOKENS, KVH * DH), 1.0, 6.0, ((0, 2), (1, 4), (2, 4)))
    doc_lengths = jax.vmap(lambda own: uneven(own, DOCS, TOKENS, MOST, 2))(jax.random.split(streams_of[3], SECTIONS)).reshape((SECTIONS, DOCS)).astype(jnp.int32)
    return {"queries": queries, "keys": keys, "values": values, "doc_lengths": doc_lengths}


def one_section(query_rows, key_rows, value_rows, lengths):
    group = QH // KVH
    ends = jnp.cumsum(lengths).astype(jnp.int32)
    positions = jnp.arange(TOKENS, dtype=jnp.int32)
    doc = lax.optimization_barrier(jnp.sum((positions[:, None] >= ends[None, :]).astype(jnp.int32), axis=1)).astype(jnp.int32)
    doc_len = lengths[doc].astype(jnp.float32)
    scale = jnp.maximum(1.0, jnp.log(doc_len) / math.log(float(LOGN_BASE)))
    queries = query_rows.reshape(TOKENS, KVH, group, DH)
    keys_f = key_rows.reshape(TOKENS, KVH, DH).astype(jnp.float32)
    values_f = value_rows.reshape(TOKENS, KVH, DH).astype(jnp.float32)
    block = min(TOKENS, 256)
    inv = 1.0 / math.sqrt(DH)

    def one_block(index):
        start = (index * block).astype(jnp.int32)
        query_block = lax.dynamic_slice_in_dim(queries, start, block, 0).astype(jnp.float32)
        pos_block = lax.dynamic_slice_in_dim(positions, start, block, 0)
        doc_block = lax.dynamic_slice_in_dim(doc, start, block, 0)
        scale_block = lax.dynamic_slice_in_dim(scale, start, block, 0)
        score = jnp.einsum('qhgd,khd->hgqk', query_block, keys_f)
        score = score * (scale_block * inv)[None, None, :, None]
        allowed = (doc_block[:, None] == doc[None, :]) & (positions[None, :] <= pos_block[:, None])
        score = jnp.where(allowed[None, None], score, -1e+30)
        top = lax.optimization_barrier(jnp.max(score, axis=-1, keepdims=True))
        weight = jnp.where(allowed[None, None], jnp.exp(score - top), 0.0)
        total = lax.optimization_barrier(jnp.sum(weight, axis=-1))
        rounded = lax.optimization_barrier(weight.astype(jnp.bfloat16)).astype(jnp.float32)
        summed = jnp.einsum('hgqk,khd->qhgd', rounded, values_f)
        result = summed / jnp.transpose(total, (2, 0, 1))[..., None]
        return result.astype(jnp.bfloat16).reshape(block, QH * DH)
    blocks = lax.map(one_block, jnp.arange(TOKENS // block, dtype=jnp.int32))
    return blocks.reshape(TOKENS, QH * DH)

def reference(queries, keys, values, doc_lengths):
    outputs = []
    for section in range(SECTIONS):
        outputs.append(one_section(queries[section], keys[section], values[section], doc_lengths[section]))
    attended = jnp.stack(outputs, axis=0)
    passed = jnp.roll(attended, 1, axis=0)
    return (attended, passed)
```

```python
import functools
import math

import jax
import jax.numpy as jnp
from jax import lax
from jax.experimental import pallas as pl
from jax.experimental.pallas import tpu as pltpu
from jax.sharding import PartitionSpec as P

DH = 128
DOCS = 16
MESH = pl.DeviceIdType.MESH
LOG2E = 1.4426950408889634
GROUP = 2


def kernel(
    dims,
    q_hbm, k_hbm, v_hbm, lengths,
    own_hbm, moved_hbm,
    q, k, v, score, bias, result,
    load_sem, kv_send, kv_recv, row_send, row_recv, own_sem, pass_send, pass_recv,
):
    sections, cycle, split, rows, heads, hops = dims
    s, p, m = lax.axis_index("section"), lax.axis_index("ctx"), lax.axis_index("mp")
    after = lax.rem(s + 1, sections)
    width = heads * DH
    part = rows // split
    groups = heads // GROUP
    span = GROUP * DH

    def load(i):
        pairs = ((k_hbm.at[0], k.at[pl.ds(0, rows)]), (v_hbm.at[0], v.at[pl.ds(0, rows)]), (q_hbm.at[0], q))
        return pltpu.make_async_copy(*pairs[i], load_sem.at[i])

    def shift(d, i):
        buf, first = ((k, k_hbm), (v, v_hbm))[i]
        src = first.at[0] if d == 0 else buf.at[pl.ds(d * rows, rows)]
        return pltpu.make_async_remote_copy(
            src_ref=src,
            dst_ref=buf.at[pl.ds((d + 1) * rows, rows)],
            send_sem=kv_send.at[d, i],
            recv_sem=kv_recv.at[d, i],
            device_id={"ctx": p + 1},
            device_id_type=MESH,
        )

    def place(holder, g):
        return pl.ds(pl.multiple_of(holder * width + g * span, DH), span)

    def spread(g, i):
        to = lax.rem(m + i, split)
        return pltpu.make_async_remote_copy(
            src_ref=result.at[pl.ds(pl.multiple_of(to * part, 16), part), pl.ds(g * span, span)],
            dst_ref=own_hbm.at[0, :, place(m, g)],
            send_sem=row_send.at[g, i - 1],
            recv_sem=row_recv.at[g, i - 1],
            device_id={"mp": to},
            device_id_type=MESH,
        )

    def arrive(g, i):
        cols = place(lax.rem(m + split - i, split), g)
        return pltpu.make_async_remote_copy(
            src_ref=own_hbm.at[0, :, cols],
            dst_ref=own_hbm.at[0, :, cols],
            send_sem=row_send.at[g, i - 1],
            recv_sem=row_recv.at[g, i - 1],
            device_id={"mp": lax.rem(m + i, split)},
            device_id_type=MESH,
        )

    def own_rows(g):
        return result.at[pl.ds(pl.multiple_of(m * part, 16), part), pl.ds(g * span, span)]

    def keep(g):
        return pltpu.make_async_copy(own_rows(g), own_hbm.at[0, :, place(m, g)], own_sem.at[g])

    def hand(g, i):
        cols = place(lax.rem(m + split - i, split), g)
        return pltpu.make_async_remote_copy(
            src_ref=own_rows(g) if i == 0 else own_hbm.at[0, :, cols],
            dst_ref=moved_hbm.at[0, :, cols],
            send_sem=pass_send.at[g, i],
            recv_sem=pass_recv.at[g, i],
            device_id={"section": after},
            device_id_type=MESH,
        )

    for i in range(3):
        load(i).start()

    barrier = pltpu.get_barrier_semaphore()

    def greet(where):
        pl.semaphore_signal(barrier, inc=1, device_id=where, device_id_type=MESH)

    pl.when(p < cycle - 1)(lambda: greet({"ctx": p + 1}))
    pl.when(p > 0)(lambda: greet({"ctx": p - 1}))
    for i in range(1, split):
        greet({"mp": lax.rem(m + i, split)})
    greet({"section": after})
    met = split
    if sections > 2:
        greet({"section": lax.rem(s + sections - 1, sections)})
        met += 1
    inside = (p > 0) & (p < cycle - 1)
    pl.when(inside)(lambda: pl.semaphore_wait(barrier, met + 2))
    pl.when(jnp.logical_not(inside))(lambda: pl.semaphore_wait(barrier, met + 1))

    @pl.when(p < cycle - 1)
    def _():
        shift(0, 0).start()
        shift(0, 1).start()

    for d in range(1, hops + 1):
        @pl.when(p < d)
        def _(d=d):
            k[pl.ds(d * rows, rows), :] = jnp.zeros((rows, DH), k.dtype)
            v[pl.ds(d * rows, rows), :] = jnp.zeros((rows, DH), v.dtype)

    t = p * rows + lax.broadcasted_iota(jnp.int32, (rows, 1), 0)
    begin = jnp.zeros((rows, 1), jnp.int32)
    finish = jnp.full((rows, 1), rows * cycle, jnp.int32)
    end = jnp.int32(0)
    for j in range(DOCS):
        end = end + lengths[0, j]
        past = t >= end
        begin = jnp.where(past, end, begin)
        finish = jnp.where(past, finish, jnp.minimum(finish, end))
    length = (finish - begin).astype(jnp.float32)
    factor = jnp.maximum(1.0, jnp.log(length) / math.log(float(rows * cycle // 16))) * (
        LOG2E / math.sqrt(DH)
    )
    for d in range(hops + 1):
        u = (p - d) * rows + lax.broadcasted_iota(jnp.int32, (rows, rows), 1)
        bias[:, d * rows:(d + 1) * rows] = jnp.where((u >= begin) & (u <= t), 0.0, -1e30)

    load(2).wait()
    for d in range(hops + 1):
        if d == 0:
            load(0).wait()
            load(1).wait()
        else:
            @pl.when(p >= d)
            def _(d=d):
                shift(d - 1, 0).wait_recv()
                if d < hops:
                    pl.when(p < cycle - 1)(lambda: shift(d, 0).start())
                shift(d - 1, 1).wait_recv()
                if d < hops:
                    pl.when(p < cycle - 1)(lambda: shift(d, 1).start())

        def raw(h, _, d=d):
            q_h = q[:, pl.ds(pl.multiple_of(h * DH, DH), DH)]
            prod = lax.dot_general(
                q_h, k[pl.ds(d * rows, rows), :], (((1,), (1,)), ((), ())),
                preferred_element_type=jnp.float32,
            )
            score[h, :, pl.ds(d * rows, rows)] = prod + bias[:, d * rows:(d + 1) * rows]
            return 0

        lax.fori_loop(0, heads, raw, 0, unroll=hops <= 4)

    def attend(h):
        x = score[h]
        top = jnp.max(x, axis=1, keepdims=True)
        weight = jnp.exp2((x - top) * factor)
        total = jnp.sum(weight, axis=1, keepdims=True)
        out = jnp.dot(weight.astype(jnp.bfloat16), v[...], preferred_element_type=jnp.float32)
        result[:, h * DH:(h + 1) * DH] = (out * (1.0 / total)).astype(jnp.bfloat16)

    def relay(g):
        for i in range(1, split):
            arrive(g, i).wait_recv()
            hand(g, i).start()

    for g in range(groups):
        for h in range(g * GROUP, (g + 1) * GROUP):
            attend(h)
        for i in range(1, split):
            spread(g, i).start()
        hand(g, 0).start()
        keep(g).start()
        if g > 0:
            relay(g - 1)
    relay(groups - 1)

    for d in range(hops):
        @pl.when((p >= d) & (p < cycle - 1))
        def _(d=d):
            shift(d, 0).wait_send()
            shift(d, 1).wait_send()
    for g in range(groups):
        keep(g).wait()
        for i in range(1, split):
            spread(g, i).wait_send()
        for i in range(split):
            hand(g, i).wait_send()
            hand(g, i).wait_recv()


def body(sections, cycle, split, queries, keys, values, doc_lengths):
    rows, width = queries.shape[1:]
    heads = width // DH
    assert keys.shape[2] == DH
    hops = min(cycle - 1, cycle // 2)
    span = (hops + 1) * rows
    groups = heads // GROUP
    part = rows // split
    out = jax.ShapeDtypeStruct((1, part, width * split), jnp.bfloat16)
    dma = pltpu.SemaphoreType.DMA
    hbm = pl.BlockSpec(memory_space=pl.ANY)
    return pl.pallas_call(
        functools.partial(kernel, (sections, cycle, split, rows, heads, hops)),
        out_shape=(out, out),
        in_specs=[hbm, hbm, hbm, pl.BlockSpec(memory_space=pltpu.SMEM)],
        out_specs=(hbm, hbm),
        scratch_shapes=[
            pltpu.VMEM((rows, width), jnp.bfloat16),
            pltpu.VMEM((span, DH), jnp.bfloat16),
            pltpu.VMEM((span, DH), jnp.bfloat16),
            pltpu.VMEM((heads, rows, span), jnp.float32),
            pltpu.VMEM((rows, span), jnp.float32),
            pltpu.VMEM((rows, width), jnp.bfloat16),
            dma((3,)),
            dma((hops, 2)),
            dma((hops, 2)),
            dma((groups, split - 1)),
            dma((groups, split - 1)),
            dma((groups,)),
            dma((groups, split)),
            dma((groups, split)),
        ],
        compiler_params=pltpu.CompilerParams(
            collective_id=0, has_side_effects=True, vmem_limit_bytes=60 * 2**20
        ),
        name="packed_attention",
    )(queries, keys, values, doc_lengths)


def solution(mesh):
    sizes = (mesh.shape["section"], mesh.shape["ctx"], mesh.shape["mp"])
    return jax.shard_map(
        functools.partial(body, *sizes),
        mesh=mesh,
        in_specs=(
            P("section", "ctx", "mp"),
            P("section", "ctx", "mp"),
            P("section", "ctx", "mp"),
            P("section", None),
        ),
        out_specs=(P("section", ("ctx", "mp"), None), P("section", ("ctx", "mp"), None)),
        check_vma=False,
    )
```

```python
import functools
import math

import jax
import jax.numpy as jnp
from jax import lax
from jax.experimental import pallas as pl
from jax.experimental.pallas import tpu as pltpu
from jax.sharding import PartitionSpec as P

DH = 128
DOCS = 16
MESH = pl.DeviceIdType.MESH
LOG2E = 1.4426950408889634
GROUP = 2


def kernel(
    dims,
    q_hbm, k_hbm, v_hbm, lengths,
    own_hbm, moved_hbm,
    q, k, v, score, bias, result,
    load_sem, kv_send, kv_recv, row_send, row_recv, own_sem, pass_send, pass_recv,
):
    sections, cycle, split, rows, heads, hops = dims
    s, p, m = lax.axis_index("section"), lax.axis_index("ctx"), lax.axis_index("mp")
    after = lax.rem(s + 1, sections)
    width = heads * DH
    part = rows // split
    groups = heads // GROUP
    span = GROUP * DH

    def load(i):
        pairs = ((k_hbm.at[0], k.at[pl.ds(0, rows)]), (v_hbm.at[0], v.at[pl.ds(0, rows)]), (q_hbm.at[0], q))
        return pltpu.make_async_copy(*pairs[i], load_sem.at[i])

    def shift(d, i):
        buf, first = ((k, k_hbm), (v, v_hbm))[i]
        src = first.at[0] if d == 0 else buf.at[pl.ds(d * rows, rows)]
        return pltpu.make_async_remote_copy(
            src_ref=src,
            dst_ref=buf.at[pl.ds((d + 1) * rows, rows)],
            send_sem=kv_send.at[d, i],
            recv_sem=kv_recv.at[d, i],
            device_id={"ctx": p + 1},
            device_id_type=MESH,
        )

    def place(holder, g):
        return pl.ds(pl.multiple_of(holder * width + g * span, DH), span)

    def spread(g, i):
        to = lax.rem(m + i, split)
        return pltpu.make_async_remote_copy(
            src_ref=result.at[pl.ds(pl.multiple_of(to * part, 16), part), pl.ds(g * span, span)],
            dst_ref=own_hbm.at[0, :, place(m, g)],
            send_sem=row_send.at[g, i - 1],
            recv_sem=row_recv.at[g, i - 1],
            device_id={"mp": to},
            device_id_type=MESH,
        )

    def own_rows(g):
        return result.at[pl.ds(pl.multiple_of(m * part, 16), part), pl.ds(g * span, span)]

    def keep(g):
        return pltpu.make_async_copy(own_rows(g), own_hbm.at[0, :, place(m, g)], own_sem.at[g])

    def hand(g, i):
        to = lax.rem(m + i, split)
        return pltpu.make_async_remote_copy(
            src_ref=result.at[pl.ds(pl.multiple_of(to * part, 16), part), pl.ds(g * span, span)],
            dst_ref=moved_hbm.at[0, :, place(m, g)],
            send_sem=pass_send.at[g, i],
            recv_sem=pass_recv.at[g, i],
            device_id={"section": after, "mp": to},
            device_id_type=MESH,
        )

    for i in range(3):
        load(i).start()

    barrier = pltpu.get_barrier_semaphore()

    def greet(where):
        pl.semaphore_signal(barrier, inc=1, device_id=where, device_id_type=MESH)

    pl.when(p < cycle - 1)(lambda: greet({"ctx": p + 1}))
    pl.when(p > 0)(lambda: greet({"ctx": p - 1}))
    for i in range(1, split):
        greet({"mp": lax.rem(m + i, split)})
    for i in range(split):
        greet({"section": after, "mp": lax.rem(m + i, split)})
    met = 2 * split - 1
    if sections > 2:
        before = lax.rem(s + sections - 1, sections)
        for i in range(split):
            greet({"section": before, "mp": lax.rem(m + i, split)})
        met += split
    inside = (p > 0) & (p < cycle - 1)
    pl.when(inside)(lambda: pl.semaphore_wait(barrier, met + 2))
    pl.when(jnp.logical_not(inside))(lambda: pl.semaphore_wait(barrier, met + 1))

    @pl.when(p < cycle - 1)
    def _():
        shift(0, 0).start()
        shift(0, 1).start()

    for d in range(1, hops + 1):
        @pl.when(p < d)
        def _(d=d):
            k[pl.ds(d * rows, rows), :] = jnp.zeros((rows, DH), k.dtype)
            v[pl.ds(d * rows, rows), :] = jnp.zeros((rows, DH), v.dtype)

    t = p * rows + lax.broadcasted_iota(jnp.int32, (rows, 1), 0)
    begin = jnp.zeros((rows, 1), jnp.int32)
    finish = jnp.full((rows, 1), rows * cycle, jnp.int32)
    end = jnp.int32(0)
    for j in range(DOCS):
        end = end + lengths[0, j]
        past = t >= end
        begin = jnp.where(past, end, begin)
        finish = jnp.where(past, finish, jnp.minimum(finish, end))
    length = (finish - begin).astype(jnp.float32)
    factor = jnp.maximum(1.0, jnp.log(length) / math.log(float(rows * cycle // 16))) * (
        LOG2E / math.sqrt(DH)
    )
    for d in range(hops + 1):
        u = (p - d) * rows + lax.broadcasted_iota(jnp.int32, (rows, rows), 1)
        bias[:, d * rows:(d + 1) * rows] = jnp.where((u >= begin) & (u <= t), 0.0, -1e30)

    load(2).wait()
    for d in range(hops + 1):
        if d == 0:
            load(0).wait()
            load(1).wait()
        else:
            @pl.when(p >= d)
            def _(d=d):
                shift(d - 1, 0).wait_recv()
                if d < hops:
                    pl.when(p < cycle - 1)(lambda: shift(d, 0).start())
                shift(d - 1, 1).wait_recv()
                if d < hops:
                    pl.when(p < cycle - 1)(lambda: shift(d, 1).start())

        def raw(h, _, d=d):
            q_h = q[:, pl.ds(pl.multiple_of(h * DH, DH), DH)]
            prod = lax.dot_general(
                q_h, k[pl.ds(d * rows, rows), :], (((1,), (1,)), ((), ())),
                preferred_element_type=jnp.float32,
            )
            score[h, :, pl.ds(d * rows, rows)] = prod + bias[:, d * rows:(d + 1) * rows]
            return 0

        lax.fori_loop(0, heads, raw, 0, unroll=hops <= 4)

    def attend(h):
        x = score[h]
        top = jnp.max(x, axis=1, keepdims=True)
        weight = jnp.exp2((x - top) * factor)
        total = jnp.sum(weight, axis=1, keepdims=True)
        out = jnp.dot(weight.astype(jnp.bfloat16), v[...], preferred_element_type=jnp.float32)
        result[:, h * DH:(h + 1) * DH] = (out * (1.0 / total)).astype(jnp.bfloat16)

    for g in range(groups):
        for h in range(g * GROUP, (g + 1) * GROUP):
            attend(h)
        for i in range(split):
            hand(g, i).start()
        for i in range(1, split):
            spread(g, i).start()
        keep(g).start()

    for d in range(hops):
        @pl.when((p >= d) & (p < cycle - 1))
        def _(d=d):
            shift(d, 0).wait_send()
            shift(d, 1).wait_send()
    for g in range(groups):
        keep(g).wait()
        for i in range(1, split):
            spread(g, i).wait_send()
            spread(g, i).wait_recv()
        for i in range(split):
            hand(g, i).wait_send()
            hand(g, i).wait_recv()


def body(sections, cycle, split, queries, keys, values, doc_lengths):
    rows, width = queries.shape[1:]
    heads = width // DH
    assert keys.shape[2] == DH
    hops = min(cycle - 1, cycle // 2)
    span = (hops + 1) * rows
    groups = heads // GROUP
    part = rows // split
    out = pltpu.VMEM((1, part, width * split), jnp.bfloat16)
    dma = pltpu.SemaphoreType.DMA
    hbm = pl.BlockSpec(memory_space=pl.ANY)
    return pl.pallas_call(
        functools.partial(kernel, (sections, cycle, split, rows, heads, hops)),
        out_shape=(out, out),
        in_specs=[hbm, hbm, hbm, pl.BlockSpec(memory_space=pltpu.SMEM)],
        out_specs=(pl.BlockSpec(memory_space=pltpu.VMEM),) * 2,
        scratch_shapes=[
            pltpu.VMEM((rows, width), jnp.bfloat16),
            pltpu.VMEM((span, DH), jnp.bfloat16),
            pltpu.VMEM((span, DH), jnp.bfloat16),
            pltpu.VMEM((heads, rows, span), jnp.float32),
            pltpu.VMEM((rows, span), jnp.float32),
            pltpu.VMEM((rows, width), jnp.bfloat16),
            dma((3,)),
            dma((hops, 2)),
            dma((hops, 2)),
            dma((groups, split - 1)),
            dma((groups, split - 1)),
            dma((groups,)),
            dma((groups, split)),
            dma((groups, split)),
        ],
        compiler_params=pltpu.CompilerParams(
            collective_id=0, has_side_effects=True, vmem_limit_bytes=60 * 2**20
        ),
        name="packed_attention",
    )(queries, keys, values, doc_lengths)


def solution(mesh):
    sizes = (mesh.shape["section"], mesh.shape["ctx"], mesh.shape["mp"])
    return jax.shard_map(
        functools.partial(body, *sizes),
        mesh=mesh,
        in_specs=(
            P("section", "ctx", "mp"),
            P("section", "ctx", "mp"),
            P("section", "ctx", "mp"),
            P("section", None),
        ),
        out_specs=(P("section", ("ctx", "mp"), None), P("section", ("ctx", "mp"), None)),
        check_vma=False,
    )
```

```python
import functools
import math

import jax
import jax.numpy as jnp
from jax import lax
from jax.experimental import pallas as pl
from jax.experimental.pallas import tpu as pltpu
from jax.sharding import PartitionSpec as P

DH = 128
DOCS = 16
MESH = pl.DeviceIdType.MESH
LOG2E = 1.4426950408889634
GROUP = 4


def kernel(
    dims,
    q_hbm, k_hbm, v_hbm, lengths,
    own_hbm, moved_hbm,
    q, k, v, score, soft, bias, result,
    load_sem, kv_send, kv_recv, row_send, row_recv, own_sem, pass_send, pass_recv,
):
    sections, cycle, split, rows, heads, hops = dims
    s, p, m = lax.axis_index("section"), lax.axis_index("ctx"), lax.axis_index("mp")
    after = lax.rem(s + 1, sections)
    width = heads * DH
    part = rows // split
    groups = heads // GROUP
    span = GROUP * DH

    def load(i):
        pairs = ((k_hbm.at[0], k.at[pl.ds(0, rows)]), (v_hbm.at[0], v.at[pl.ds(0, rows)]), (q_hbm.at[0], q))
        return pltpu.make_async_copy(*pairs[i], load_sem.at[i])

    def shift(d, i):
        buf, first = ((k, k_hbm), (v, v_hbm))[i]
        src = first.at[0] if d == 0 else buf.at[pl.ds(d * rows, rows)]
        return pltpu.make_async_remote_copy(
            src_ref=src,
            dst_ref=buf.at[pl.ds((d + 1) * rows, rows)],
            send_sem=kv_send.at[d, i],
            recv_sem=kv_recv.at[d, i],
            device_id={"ctx": p + 1},
            device_id_type=MESH,
        )

    def place(holder, g):
        return pl.ds(pl.multiple_of(holder * width + g * span, DH), span)

    def spread(g, i):
        to = lax.rem(m + i, split)
        return pltpu.make_async_remote_copy(
            src_ref=result.at[pl.ds(pl.multiple_of(to * part, 16), part), pl.ds(g * span, span)],
            dst_ref=own_hbm.at[0, :, place(m, g)],
            send_sem=row_send.at[g, i - 1],
            recv_sem=row_recv.at[g, i - 1],
            device_id={"mp": to},
            device_id_type=MESH,
        )

    def own_rows(g):
        return result.at[pl.ds(pl.multiple_of(m * part, 16), part), pl.ds(g * span, span)]

    def keep(g):
        return pltpu.make_async_copy(own_rows(g), own_hbm.at[0, :, place(m, g)], own_sem.at[g])

    def hand(g, i):
        to = lax.rem(m + i, split)
        return pltpu.make_async_remote_copy(
            src_ref=result.at[pl.ds(pl.multiple_of(to * part, 16), part), pl.ds(g * span, span)],
            dst_ref=moved_hbm.at[0, :, place(m, g)],
            send_sem=pass_send.at[g, i],
            recv_sem=pass_recv.at[g, i],
            device_id={"section": after, "mp": to},
            device_id_type=MESH,
        )

    for i in range(3):
        load(i).start()

    barrier = pltpu.get_barrier_semaphore()

    def greet(where):
        pl.semaphore_signal(barrier, inc=1, device_id=where, device_id_type=MESH)

    pl.when(p < cycle - 1)(lambda: greet({"ctx": p + 1}))
    pl.when(p > 0)(lambda: greet({"ctx": p - 1}))
    for i in range(1, split):
        greet({"mp": lax.rem(m + i, split)})
    for i in range(split):
        greet({"section": after, "mp": lax.rem(m + i, split)})
    met = 2 * split - 1
    if sections > 2:
        before = lax.rem(s + sections - 1, sections)
        for i in range(split):
            greet({"section": before, "mp": lax.rem(m + i, split)})
        met += split
    inside = (p > 0) & (p < cycle - 1)
    pl.when(inside)(lambda: pl.semaphore_wait(barrier, met + 2))
    pl.when(jnp.logical_not(inside))(lambda: pl.semaphore_wait(barrier, met + 1))

    @pl.when(p < cycle - 1)
    def _():
        shift(0, 0).start()
        shift(0, 1).start()

    for d in range(1, hops + 1):
        @pl.when(p < d)
        def _(d=d):
            k[pl.ds(d * rows, rows), :] = jnp.zeros((rows, DH), k.dtype)
            v[pl.ds(d * rows, rows), :] = jnp.zeros((rows, DH), v.dtype)

    t = p * rows + lax.broadcasted_iota(jnp.int32, (rows, 1), 0)
    begin = jnp.zeros((rows, 1), jnp.int32)
    finish = jnp.full((rows, 1), rows * cycle, jnp.int32)
    end = jnp.int32(0)
    for j in range(DOCS):
        end = end + lengths[0, j]
        past = t >= end
        begin = jnp.where(past, end, begin)
        finish = jnp.where(past, finish, jnp.minimum(finish, end))
    length = (finish - begin).astype(jnp.float32)
    factor = jnp.maximum(1.0, jnp.log(length) / math.log(float(rows * cycle // 16))) * (
        LOG2E / math.sqrt(DH)
    )
    for d in range(hops + 1):
        u = (p - d) * rows + lax.broadcasted_iota(jnp.int32, (rows, rows), 1)
        bias[:, d * rows:(d + 1) * rows] = jnp.where((u >= begin) & (u <= t), 0.0, -1e30)

    staged = hops <= 4
    load(2).wait()
    load(0).wait()
    load(1).wait()

    def raw(h, d, count):
        prod = lax.dot_general(
            q[:, h * DH:(h + 1) * DH], k[pl.ds(d * rows, count * rows), :], (((1,), (1,)), ((), ())),
            preferred_element_type=jnp.float32,
        )
        return prod + bias[:, d * rows:(d + count) * rows]

    def ready(d, i):
        if d > 0:
            @pl.when(p >= d)
            def _():
                shift(d - 1, i).wait_recv()
                if d < hops:
                    pl.when(p < cycle - 1)(lambda: shift(d, i).start())

    def soften(x):
        top = jnp.max(x, axis=1, keepdims=True)
        weight = jnp.exp2((x - top) * factor)
        return weight.astype(jnp.bfloat16), 1.0 / jnp.sum(weight, axis=1, keepdims=True)

    inverse = []
    for d in range(hops + 1):
        ready(d, 0)
        if staged and d < hops:
            for h in range(heads):
                score[h, :, d * rows:(d + 1) * rows] = raw(h, d, 1)
        if staged and d == hops:
            for h in range(heads):
                x = jnp.concatenate([score[h], raw(h, d, 1)], axis=1)
                soft[h], over = soften(x)
                inverse.append(over)
        ready(d, 1)

    def attend(h):
        if staged:
            weight, over = soft[h], inverse[h]
        else:
            weight, over = soften(raw(h, 0, hops + 1))
        out = jnp.dot(weight, v[...], preferred_element_type=jnp.float32)
        result[:, h * DH:(h + 1) * DH] = (out * over).astype(jnp.bfloat16)

    for g in range(groups):
        for h in range(g * GROUP, (g + 1) * GROUP):
            attend(h)
        for i in range(split):
            hand(g, i).start()
        for i in range(1, split):
            spread(g, i).start()
        keep(g).start()

    for d in range(hops):
        @pl.when((p >= d) & (p < cycle - 1))
        def _(d=d):
            shift(d, 0).wait_send()
            shift(d, 1).wait_send()
    for g in range(groups):
        keep(g).wait()
        for i in range(1, split):
            spread(g, i).wait_send()
            spread(g, i).wait_recv()
        for i in range(split):
            hand(g, i).wait_send()
            hand(g, i).wait_recv()


def body(sections, cycle, split, queries, keys, values, doc_lengths):
    rows, width = queries.shape[1:]
    heads = width // DH
    assert keys.shape[2] == DH
    hops = min(cycle - 1, cycle // 2)
    span = (hops + 1) * rows
    groups = heads // GROUP
    part = rows // split
    out = pltpu.VMEM((1, part, width * split), jnp.bfloat16)
    dma = pltpu.SemaphoreType.DMA
    hbm = pl.BlockSpec(memory_space=pl.ANY)
    return pl.pallas_call(
        functools.partial(kernel, (sections, cycle, split, rows, heads, hops)),
        out_shape=(out, out),
        in_specs=[hbm, hbm, hbm, pl.BlockSpec(memory_space=pltpu.SMEM)],
        out_specs=(pl.BlockSpec(memory_space=pltpu.VMEM),) * 2,
        scratch_shapes=[
            pltpu.VMEM((rows, width), jnp.bfloat16),
            pltpu.VMEM((span, DH), jnp.bfloat16),
            pltpu.VMEM((span, DH), jnp.bfloat16),
            pltpu.VMEM((heads, rows, span - rows) if hops <= 4 else (8, DH), jnp.float32),
            pltpu.VMEM((heads, rows, span) if hops <= 4 else (16, DH), jnp.bfloat16),
            pltpu.VMEM((rows, span), jnp.float32),
            pltpu.VMEM((rows, width), jnp.bfloat16),
            dma((3,)),
            dma((hops, 2)),
            dma((hops, 2)),
            dma((groups, split - 1)),
            dma((groups, split - 1)),
            dma((groups,)),
            dma((groups, split)),
            dma((groups, split)),
        ],
        compiler_params=pltpu.CompilerParams(
            collective_id=0, has_side_effects=True, vmem_limit_bytes=60 * 2**20
        ),
        name="packed_attention",
    )(queries, keys, values, doc_lengths)


def solution(mesh):
    sizes = (mesh.shape["section"], mesh.shape["ctx"], mesh.shape["mp"])
    return jax.shard_map(
        functools.partial(body, *sizes),
        mesh=mesh,
        in_specs=(
            P("section", "ctx", "mp"),
            P("section", "ctx", "mp"),
            P("section", "ctx", "mp"),
            P("section", None),
        ),
        out_specs=(P("section", ("ctx", "mp"), None), P("section", ("ctx", "mp"), None)),
        check_vma=False,
    )
```
